256 devices in a mesh: row: 8 (over z), col: 32 (over x, y, core).
Axes of the slice: x: 4, y: 4, z: 8, core: 2. Of those that a mesh axis runs over, the one named last changes fastest.
Arguments:
- gradient: bfloat16 [8192, 53248], P('row', 'col'), may hold values from -6 to 6
- momentum: bfloat16 [8192, 53248], P('row', 'col'), may hold values from -8 to 8
- right_factor: bfloat16 [53248, 512], P('col'), may hold values from -0.02734375 to 0.02734375
Outputs:
- momentum_next: bfloat16 [8192, 53248], P('row', 'col')
- right_next: bfloat16 [53248, 512], P('col')
- update: bfloat16 [8192, 53248], P('row', 'col')
The draws below stay inside these ranges and needn't reach their ends.
All inputs are finite; a program needn't handle non-finite values.
Results may differ from the reference program's by a relative error of at most 0.015.
Values may be sent and summed in bfloat16 or wider, within the bound.
No kernel may reach another device: no remote copies, remote signals or barrier semaphores. Data moves between devices by JAX's collectives and lax.ppermute only.
A program may use at most 64 MiB of HBM per device.

```python
import jax
import jax.numpy as jnp
from jax import lax

RANK = 512
ROWS = 8192
COLS = 53248


def outer_terms(key, weight):
    key_left, key_right = jax.random.split(key)
    left_ints = jax.random.randint(key_left, (ROWS, 8), -96, 97).astype(jnp.float32) / 32.0
    right_ints = jax.random.randint(key_right, (COLS, 8), -96, 97).astype(jnp.float32) / 32.0
    total = jnp.zeros((ROWS, COLS), jnp.float32)
    for which in range(8):
        level = weight * 2.0 ** (-(which // 2))
        total = total + (level * left_ints[:, which])[:, None] * right_ints[:, which][None, :]
    return total


def column_scale(low, high):
    place = jnp.arange(COLS).astype(jnp.float32) / (COLS - 1)
    return (low + (high - low) * place)[None, :]


def draw_momentum(key, part):
    key = jax.random.fold_in(key, 11)
    key_terms, key_noise = jax.random.split(key)
    noise = jax.random.normal(key_noise, (ROWS, COLS), jnp.float32)
    field = (outer_terms(key_terms, 0.5) + noise) * column_scale(0.5, 3.0)
    return jnp.clip(field, -8.0, 8.0).astype(jnp.bfloat16)


def levels(stream_key, dims, cuts, smallest, largest):
    factor_of, own = 1.0, jax.random.fold_in(stream_key, 6)
    for axis_at, blocks in cuts:
        draws = jnp.exp(jax.random.uniform(jax.random.fold_in(own, axis_at), (blocks,), jnp.float32, smallest / len(cuts), largest / len(cuts)))
        factor_of = factor_of * jnp.repeat(draws, dims[axis_at] // blocks).reshape([-1 if axis == axis_at else 1 for axis in range(len(dims))])
    return factor_of


def bell_draw(own_key, shape, deviation, reach, cuts=(), kind=jnp.bfloat16):
    level = levels(own_key, shape, cuts, -0.22, 0.18) if cuts else 1.0
    result = jax.random.normal(own_key, shape, jnp.float32) * deviation * level
    return jnp.minimum(jnp.maximum(result, -reach), reach).astype(kind)


def setup_inputs(seed: int = 0) -> dict:
    splits = jax.random.split(jax.random.key(seed), 4)
    return {
        "gradient": bell_draw(splits[0], (ROWS, COLS), 1.0, 6.0, ((0, 8), (1, 32))),
        "momentum": draw_momentum(jax.random.fold_in(splits[3], 71), 0),
        "right_factor": bell_draw(splits[2], (COLS, RANK), COLS ** -0.5, 0.02734375, ((0, 32),)),
    }


def reference(gradient, momentum, right_factor):
    blended = (momentum.astype(jnp.float32) + gradient.astype(jnp.float32)).astype(jnp.bfloat16)
    left = jnp.dot(blended.astype(jnp.float32), right_factor.astype(jnp.float32), preferred_element_type=jnp.float32)
    gram = jnp.dot(left.T.astype(jnp.float32), left.astype(jnp.float32), precision=lax.Precision.HIGHEST, preferred_element_type=jnp.float32)
    chol = jnp.linalg.cholesky(gram)
    left_orth = jax.scipy.linalg.solve_triangular(chol, left.T, lower=True).T.astype(jnp.bfloat16)
    right = jnp.einsum('ij,ik->jk', blended.astype(jnp.float32), left_orth.astype(jnp.float32), preferred_element_type=jnp.float32)
    colsq = lax.optimization_barrier(jnp.sum(right * right, axis=0))
    right_bf = right.astype(jnp.bfloat16)
    right_next = (right_bf.astype(jnp.float32) / jnp.sqrt(colsq + 1e-06)).astype(jnp.bfloat16)
    correction = jnp.einsum('ik,jk->ij', left_orth.astype(jnp.float32), right_bf.astype(jnp.float32), preferred_element_type=jnp.float32)
    momentum_next = (blended.astype(jnp.float32) - 0.1 * correction).astype(jnp.bfloat16)
    factor = (ROWS * COLS / RANK) ** 0.5
    update = (factor * jnp.einsum('ik,jk->ij', left_orth.astype(jnp.float32), right_next.astype(jnp.float32), preferred_element_type=jnp.float32)).astype(jnp.bfloat16)
    return (momentum_next, right_next, update)
```

```python
import jax
import jax.numpy as jnp
from jax import lax
from jax.experimental import pallas as pl
from jax.experimental.pallas import tpu as pltpu
from jax.sharding import Mesh, PartitionSpec as P

HI = lax.Precision.HIGHEST
TILE = 8


def diag_inverse(block):
    n = block.shape[0]
    tiles = n // TILE
    shape = (TILE, n)
    row = lax.broadcasted_iota(jnp.int32, shape, 0)
    lane = lax.broadcasted_iota(jnp.int32, shape, 1)
    s = [block[t * TILE:(t + 1) * TILE, :] for t in range(tiles)]
    x = [jnp.where(lane == row + t * TILE, 1.0, 0.0) for t in range(tiles)]
    spread = lambda v, i: jnp.broadcast_to(v[i:i + 1, :], shape)
    for p in range(tiles):
        rest = range(p + 1, tiles)
        col = [
            {t: jnp.broadcast_to(s[t][:, p * TILE + b:p * TILE + b + 1], shape) for t in range(p, tiles)}
            for b in range(TILE)
        ]
        for j in range(TILE):
            inv = lax.rsqrt(spread(col[j][p], j))
            low = {t: col[j][t] * inv for t in range(p, tiles)}
            mult = jnp.where(row > j, low[p], 0.0)
            keep = jnp.where(row == j, inv, 1.0)
            for b in range(j + 1, TILE):
                u = spread(low[p], b)
                for t in range(p, tiles):
                    col[b][t] = col[b][t] - low[t] * u
            srow = spread(s[p], j) * inv
            xrow = spread(x[p], j) * inv
            s[p] = s[p] * keep - mult * srow
            x[p] = x[p] * keep - mult * xrow
            for t in rest:
                s[t] = s[t] - low[t] * srow
                x[t] = x[t] - low[t] * xrow
    return jnp.concatenate(x, axis=0)


def chol_kernel(gram_ref, inv_ref, work):
    n = gram_ref.shape[0]
    nb = 128
    work[...] = gram_ref[...]
    r = lax.broadcasted_iota(jnp.int32, (n, n), 0)
    c = lax.broadcasted_iota(jnp.int32, (n, n), 1)
    inv_ref[...] = jnp.where(r == c, 1.0, 0.0)

    def step(k, carry):
        o = pl.multiple_of(k * nb, nb)
        here = pl.ds(o, nb)
        d = diag_inverse(work[here, here])
        u = jnp.dot(d, work[here, :], precision=HI, preferred_element_type=jnp.float32)
        lanes = lax.broadcasted_iota(jnp.int32, (nb, n), 1)
        u = jnp.where(lanes >= o + nb, u, 0.0)
        y = jnp.dot(d, inv_ref[here, :], precision=HI, preferred_element_type=jnp.float32)
        tdot = lambda a, b: lax.dot_general(a, b, (((0,), (0,)), ((), ())), precision=HI, preferred_element_type=jnp.float32)
        work[...] = work[...] - tdot(u, u)
        inv_ref[...] = inv_ref[...] - tdot(u, y)
        inv_ref[here, :] = y
        return carry

    lax.fori_loop(0, n // nb, step, 0)


def chol_inverse(gram):
    n = gram.shape[0]
    return pl.pallas_call(
        chol_kernel,
        out_shape=jax.ShapeDtypeStruct((n, n), jnp.float32),
        in_specs=[pl.BlockSpec(memory_space=pltpu.VMEM)],
        out_specs=pl.BlockSpec(memory_space=pltpu.VMEM),
        scratch_shapes=[pltpu.VMEM((n, n), jnp.float32)],
        compiler_params=pltpu.CompilerParams(vmem_limit_bytes=32 * 1024 * 1024),
        cost_estimate=pl.CostEstimate(flops=20 * 10**9, bytes_accessed=8 * n * n, transcendentals=0),
    )(gram)


CHIPS = ("x", "y")


def swap_cores(value):
    return lax.ppermute(value, "c", [(0, 1), (1, 0)])


def spread_over(value, axes, parts):
    many = jnp.broadcast_to(value[None], (parts,) + value.shape)
    return lax.all_to_all(many, axes, 0, 0, tiled=True)


def gather_over_columns(value, chips):
    mine = spread_over(value, CHIPS, chips).reshape(chips * value.shape[0], value.shape[1])
    other = swap_cores(mine)
    first = lax.axis_index("c") == 0
    return jnp.concatenate([jnp.where(first, mine, other), jnp.where(first, other, mine)])


def three_terms(value):
    high = lax.reduce_precision(value, 8, 7)
    rest = value - high
    mid = lax.reduce_precision(rest, 8, 7)
    return [t.astype(jnp.bfloat16) for t in (high, mid, rest - mid)]


def per_device(gradient, momentum, right_factor):
    rows_dev, cols_dev = gradient.shape
    rank = right_factor.shape[1]
    chips = lax.axis_size("x") * lax.axis_size("y")
    depth = lax.axis_size("z")
    core = lax.axis_index("c")
    place = (core * lax.axis_size("x") + lax.axis_index("x")) * lax.axis_size("y") + lax.axis_index("y")
    blended = (momentum.astype(jnp.float32) + gradient.astype(jnp.float32)).astype(jnp.bfloat16)
    local_left = jnp.dot(blended, right_factor, preferred_element_type=jnp.float32)
    halves = local_left.reshape(2, rows_dev // 2, rank)
    mine = lax.dynamic_index_in_dim(halves, core, 0, keepdims=False)
    other = lax.dynamic_index_in_dim(halves, 1 - core, 0, keepdims=False)
    pair = (mine + swap_cores(other)).reshape(chips, rows_dev // (2 * chips), rank)
    shard = jnp.sum(lax.all_to_all(pair, CHIPS, 0, 0, tiled=True), axis=0)
    left = gather_over_columns(shard, chips)
    wide = sum(
        lax.dot_general(blended, t, (((0,), (0,)), ((), ())), preferred_element_type=jnp.float32)
        for t in three_terms(left)
    )
    wide = lax.psum_scatter(wide, "z", scatter_dimension=0, tiled=True)
    width = rank // (2 * chips)
    part = lax.dynamic_slice(left, (0, place * width), (rows_dev, width))
    slab = lax.dot_general(part, left, (((0,), (0,)), ((), ())), precision=HI, preferred_element_type=jnp.float32)
    slab = jnp.sum(spread_over(slab, "z", depth), axis=0)
    gram = gather_over_columns(slab, chips)
    inverse = chol_inverse(gram)
    times_inverse = lambda a: lax.dot_general(
        a, inverse, (((1,), (1,)), ((), ())), precision=HI, preferred_element_type=jnp.float32
    )
    right = times_inverse(wide)
    right_bf = lax.all_gather(right.astype(jnp.bfloat16), "z", axis=0, tiled=True)
    left_orth = times_inverse(left).astype(jnp.bfloat16)
    colsq = jnp.sum(right * right, axis=0).reshape(rank // 128, 128)
    colsq = jnp.sum(spread_over(colsq, ("x", "y", "c"), 2 * chips), axis=0)
    colsq = jnp.sum(spread_over(colsq, "z", depth), axis=0).reshape(rank)
    right_next = (right_bf.astype(jnp.float32) / jnp.sqrt(colsq + 1e-06)).astype(jnp.bfloat16)
    correction = jnp.einsum("ik,jk->ij", left_orth, right_bf, preferred_element_type=jnp.float32)
    momentum_next = (blended.astype(jnp.float32) - 0.1 * correction).astype(jnp.bfloat16)
    total_rows = rows_dev * depth
    total_cols = cols_dev * 2 * chips
    factor = (total_rows * total_cols / rank) ** 0.5
    update = (
        factor * jnp.einsum("ik,jk->ij", left_orth, right_next, preferred_element_type=jnp.float32)
    ).astype(jnp.bfloat16)
    return (momentum_next, right_next, update)


def solution(mesh):
    fine = Mesh(mesh.devices.reshape(8, 4, 4, 2), ("z", "x", "y", "c"))
    col = ("x", "y", "c")
    return jax.shard_map(
        per_device,
        mesh=fine,
        in_specs=(P("z", col), P("z", col), P(col, None)),
        out_specs=(P("z", col), P(col, None), P("z", col)),
        check_vma=False,
    )
```

```python
import jax
import jax.numpy as jnp
from jax import lax
from jax.experimental import pallas as pl
from jax.experimental.pallas import tpu as pltpu
from jax.sharding import Mesh, PartitionSpec as P

HI = lax.Precision.HIGHEST
TILE = 8


def diag_inverse(block):
    n = block.shape[0]
    tiles = n // TILE
    shape = (TILE, n)
    row = lax.broadcasted_iota(jnp.int32, shape, 0)
    lane = lax.broadcasted_iota(jnp.int32, shape, 1)
    s = [block[t * TILE:(t + 1) * TILE, :] for t in range(tiles)]
    x = [jnp.where(lane == row + t * TILE, 1.0, 0.0) for t in range(tiles)]
    spread = lambda v, i: jnp.broadcast_to(v[i:i + 1, :], shape)
    for p in range(tiles):
        rest = range(p + 1, tiles)
        col = [
            {t: jnp.broadcast_to(s[t][:, p * TILE + b:p * TILE + b + 1], shape) for t in range(p, tiles)}
            for b in range(TILE)
        ]
        for j in range(TILE):
            inv = lax.rsqrt(spread(col[j][p], j))
            low = {t: col[j][t] * inv for t in range(p, tiles)}
            mult = jnp.where(row > j, low[p], 0.0)
            keep = jnp.where(row == j, inv, 1.0)
            for b in range(j + 1, TILE):
                u = spread(low[p], b)
                for t in range(p, tiles):
                    col[b][t] = col[b][t] - low[t] * u
            srow = spread(s[p], j) * inv
            xrow = spread(x[p], j) * inv
            s[p] = s[p] * keep - mult * srow
            x[p] = x[p] * keep - mult * xrow
            for t in rest:
                s[t] = s[t] - low[t] * srow
                x[t] = x[t] - low[t] * xrow
    return jnp.concatenate(x, axis=0)


def chol_kernel(gram_ref, inv_ref, work):
    n = gram_ref.shape[0]
    nb = 128
    work[...] = gram_ref[...]
    inv_ref[...] = jnp.zeros((n, n), jnp.float32)
    dot = lambda a, b: jnp.dot(a, b, precision=HI, preferred_element_type=jnp.float32)

    def finish(o, d):
        after = o + nb
        here = slice(o, after)
        inv_ref[here, here] = d
        if o:
            inv_ref[here, :o] = dot(d, inv_ref[here, :o])
        if after < n:
            u = dot(d, work[here, after:])
            ut = u.T
            work[after:, after:] = work[after:, after:] - dot(ut, u)
            inv_ref[after:, :after] = inv_ref[after:, :after] - dot(ut, inv_ref[here, :after])

    def step(k, carry):
        o = pl.multiple_of(k * nb, nb)
        d = diag_inverse(work[pl.ds(o, nb), pl.ds(o, nb)])
        for which in range(n // nb):
            pl.when(k == which)(lambda: finish(which * nb, d))
        return carry

    lax.fori_loop(0, n // nb, step, 0)

def chol_inverse(gram):
    n = gram.shape[0]
    return pl.pallas_call(
        chol_kernel,
        out_shape=jax.ShapeDtypeStruct((n, n), jnp.float32),
        in_specs=[pl.BlockSpec(memory_space=pltpu.VMEM)],
        out_specs=pl.BlockSpec(memory_space=pltpu.VMEM),
        scratch_shapes=[pltpu.VMEM((n, n), jnp.float32)],
        compiler_params=pltpu.CompilerParams(vmem_limit_bytes=16 * 1024 * 1024),
        cost_estimate=pl.CostEstimate(flops=20 * 10**9, bytes_accessed=8 * n * n, transcendentals=0),
    )(gram)


CHIPS = ("x", "y")
VMEM = 16 * 1024 * 1024
TN = (((0,), (0,)), ((), ()))
NT = (((1,), (1,)), ((), ()))


def call(kernel, out_shape, grid, in_specs, out_specs, scratch=(), flops=0, moved=0, scalars=1):
    return pl.pallas_call(
        kernel,
        out_shape=out_shape,
        grid_spec=pltpu.PrefetchScalarGridSpec(
            num_scalar_prefetch=scalars, grid=grid, in_specs=in_specs, out_specs=out_specs, scratch_shapes=list(scratch)
        ),
        compiler_params=pltpu.CompilerParams(vmem_limit_bytes=VMEM),
        cost_estimate=pl.CostEstimate(flops=flops, bytes_accessed=moved, transcendentals=0),
    )


def slab_kernel(place_ref, part_a, part_b, left_a, left_b, out_ref, scratch):
    width = out_ref.shape[0]
    scratch[...] = lax.dot_general(
        part_a[...], left_a[...], TN, precision=HI, preferred_element_type=jnp.float32
    ) + lax.dot_general(part_b[...], left_b[...], TN, precision=HI, preferred_element_type=jnp.float32)
    start = pl.multiple_of(lax.rem(place_ref[0], 128 // width) * width, width)
    out_ref[...] = scratch[pl.ds(start, width), :]


def gram_slab(place, width, left_a, left_b):
    rows, rank = left_a.shape
    part = pl.BlockSpec((rows, 128), lambda i, p: (0, p[0] // (128 // width)))
    whole = pl.BlockSpec((rows, rank), lambda i, p: (0, 0))
    return call(
        slab_kernel,
        jax.ShapeDtypeStruct((width, rank), jnp.float32),
        (1,),
        [part, part, whole, whole],
        pl.BlockSpec((width, rank), lambda i, p: (0, 0)),
        [pltpu.VMEM((128, rank), jnp.float32)],
        flops=24 * rows * 128 * rank,
        moved=10 * rows * rank,
    )(place.reshape(1), left_a, left_b, left_a, left_b)


def three_terms(value):
    high = lax.reduce_precision(value, 8, 7)
    rest = value - high
    mid = lax.reduce_precision(rest, 8, 7)
    return [t.astype(jnp.bfloat16) for t in (high, mid, rest - mid)]


def swap_cores(value):
    return lax.ppermute(value, "c", [(0, 1), (1, 0)])


def spread_over(value, axes, parts):
    many = jnp.broadcast_to(value[None], (parts,) + value.shape)
    return lax.all_to_all(many, axes, 0, 0, tiled=True)


def gather_over_chips(value, chips):
    return spread_over(value, CHIPS, chips).reshape(chips * value.shape[0], value.shape[1])


def per_device(gradient, momentum, right_factor):
    rows_dev, cols_dev = gradient.shape
    rank = right_factor.shape[1]
    chips = lax.axis_size("x") * lax.axis_size("y")
    depth = lax.axis_size("z")
    core = lax.axis_index("c")
    place = (core * lax.axis_size("x") + lax.axis_index("x")) * lax.axis_size("y") + lax.axis_index("y")
    blended = (momentum.astype(jnp.float32) + gradient.astype(jnp.float32)).astype(jnp.bfloat16)
    half = rows_dev // 2
    part_b, part_a = (
        jnp.dot(
            lax.dynamic_slice_in_dim(blended, h * half, half),
            right_factor,
            preferred_element_type=jnp.float32,
        )
        for h in (1 - core, core)
    )
    part_a = lax.optimization_barrier(part_a)
    pair = (part_a + swap_cores(part_b)).reshape(chips, rows_dev // (2 * chips), rank)
    shard = jnp.sum(lax.all_to_all(pair, CHIPS, 0, 0, tiled=True), axis=0)
    left_a = gather_over_chips(shard, chips)
    left_b = swap_cores(left_a)
    left = jnp.concatenate([jnp.where(core == 0, left_a, left_b), jnp.where(core == 0, left_b, left_a)])
    wide = sum(
        lax.dot_general(blended, t, TN, preferred_element_type=jnp.float32) for t in three_terms(left)
    )
    wide = lax.psum_scatter(wide, "z", scatter_dimension=0, tiled=True)
    slab = gram_slab(place, rank // (2 * chips), left_a, left_b)
    slab = jnp.sum(spread_over(slab, "z", depth), axis=0)
    mine = gather_over_chips(slab, chips)
    other = swap_cores(mine)
    gram = jnp.concatenate([jnp.where(core == 0, mine, other), jnp.where(core == 0, other, mine)])
    inverse = chol_inverse(gram)
    right = lax.dot_general(wide, inverse, NT, precision=HI, preferred_element_type=jnp.float32)
    colsq = jnp.sum(right * right, axis=0)
    right_bf = lax.all_gather(right.astype(jnp.bfloat16), "z", axis=0, tiled=True)
    left_orth = lax.dot_general(left, inverse, NT, precision=HI, preferred_element_type=jnp.float32).astype(jnp.bfloat16)
    colsq = colsq.reshape(rank // 128, 128)
    colsq = jnp.sum(spread_over(colsq, ("x", "y", "c"), 2 * chips), axis=0)
    colsq = jnp.sum(spread_over(colsq, "z", depth), axis=0).reshape(1, rank)
    scale = 1.0 / jnp.sqrt(colsq + 1e-06)
    right_next = (right_bf.astype(jnp.float32) * scale).astype(jnp.bfloat16)
    correction = lax.dot_general(left_orth, right_bf, NT, preferred_element_type=jnp.float32)
    momentum_next = (blended.astype(jnp.float32) - 0.1 * correction).astype(jnp.bfloat16)
    factor = (rows_dev * depth * cols_dev * 2 * chips / rank) ** 0.5
    product = lax.dot_general(left_orth, right_next, NT, preferred_element_type=jnp.float32)
    return (momentum_next, right_next, (factor * product).astype(jnp.bfloat16))


def solution(mesh):
    fine = Mesh(mesh.devices.reshape(8, 4, 4, 2), ("z", "x", "y", "c"))
    col = ("x", "y", "c")
    return jax.shard_map(
        per_device,
        mesh=fine,
        in_specs=(P("z", col), P("z", col), P(col, None)),
        out_specs=(P("z", col), P(col, None), P("z", col)),
        check_vma=False,
    )
```

```python
import jax
import jax.numpy as jnp
from jax import lax
from jax.experimental import pallas as pl
from jax.experimental.pallas import tpu as pltpu
from jax.sharding import Mesh, PartitionSpec as P

HI = lax.Precision.HIGHEST
TILE = 8


def diag_inverse(block):
    n = block.shape[0]
    tiles = n // TILE
    shape = (TILE, n)
    row = lax.broadcasted_iota(jnp.int32, shape, 0)
    lane = lax.broadcasted_iota(jnp.int32, shape, 1)
    s = [block[t * TILE:(t + 1) * TILE, :] for t in range(tiles)]
    x = [jnp.where(lane == row + t * TILE, 1.0, 0.0) for t in range(tiles)]
    spread = lambda v, i: jnp.broadcast_to(v[i:i + 1, :], shape)
    for p in range(tiles):
        rest = range(p + 1, tiles)
        col = [
            {t: jnp.broadcast_to(s[t][:, p * TILE + b:p * TILE + b + 1], shape) for t in range(p, tiles)}
            for b in range(TILE)
        ]
        for j in range(TILE):
            inv = lax.rsqrt(spread(col[j][p], j))
            low = {t: col[j][t] * inv for t in range(p, tiles)}
            mult = jnp.where(row > j, low[p], 0.0)
            keep = jnp.where(row == j, inv, 1.0)
            for b in range(j + 1, TILE):
                u = spread(low[p], b)
                for t in range(p, tiles):
                    col[b][t] = col[b][t] - low[t] * u
            srow = spread(s[p], j) * inv
            xrow = spread(x[p], j) * inv
            s[p] = s[p] * keep - mult * srow
            x[p] = x[p] * keep - mult * xrow
            for t in rest:
                s[t] = s[t] - low[t] * srow
                x[t] = x[t] - low[t] * xrow
    return jnp.concatenate(x, axis=0)


def chol_kernel(gram_ref, inv_ref, work):
    n = gram_ref.shape[0]
    nb = 128
    work[...] = gram_ref[...]
    inv_ref[...] = jnp.zeros((n, n), jnp.float32)
    dot = lambda a, b: jnp.dot(a, b, precision=HI, preferred_element_type=jnp.float32)

    def finish(o, d):
        after = o + nb
        here = slice(o, after)
        inv_ref[here, here] = d
        if o:
            inv_ref[here, :o] = dot(d, inv_ref[here, :o])
        if after < n:
            u = dot(d, work[here, after:])
            ut = u.T
            work[after:, after:] = work[after:, after:] - dot(ut, u)
            inv_ref[after:, :after] = inv_ref[after:, :after] - dot(ut, inv_ref[here, :after])

    def step(k, carry):
        o = pl.multiple_of(k * nb, nb)
        d = diag_inverse(work[pl.ds(o, nb), pl.ds(o, nb)])
        for which in range(n // nb):
            pl.when(k == which)(lambda: finish(which * nb, d))
        return carry

    lax.fori_loop(0, n // nb, step, 0)

def chol_inverse(gram):
    n = gram.shape[0]
    return pl.pallas_call(
        chol_kernel,
        out_shape=jax.ShapeDtypeStruct((n, n), jnp.float32),
        in_specs=[pl.BlockSpec(memory_space=pltpu.VMEM)],
        out_specs=pl.BlockSpec(memory_space=pltpu.VMEM),
        scratch_shapes=[pltpu.VMEM((n, n), jnp.float32)],
        compiler_params=pltpu.CompilerParams(vmem_limit_bytes=16 * 1024 * 1024),
        cost_estimate=pl.CostEstimate(flops=20 * 10**9, bytes_accessed=8 * n * n, transcendentals=0),
    )(gram)


CHIPS = ("x", "y")
VMEM = 16 * 1024 * 1024
TN = (((0,), (0,)), ((), ()))
NT = (((1,), (1,)), ((), ()))


def call(kernel, out_shape, grid, in_specs, out_specs, scratch=(), flops=0, moved=0, scalars=1, vmem=VMEM):
    return pl.pallas_call(
        kernel,
        out_shape=out_shape,
        grid_spec=pltpu.PrefetchScalarGridSpec(
            num_scalar_prefetch=scalars, grid=grid, in_specs=in_specs, out_specs=out_specs, scratch_shapes=list(scratch)
        ),
        compiler_params=pltpu.CompilerParams(vmem_limit_bytes=vmem),
        cost_estimate=pl.CostEstimate(flops=flops, bytes_accessed=moved, transcendentals=0),
    )


def slab_kernel(place_ref, part_a, part_b, left_a, left_b, out_ref, scratch):
    width = out_ref.shape[0]
    scratch[...] = lax.dot_general(
        part_a[...], left_a[...], TN, precision=HI, preferred_element_type=jnp.float32
    ) + lax.dot_general(part_b[...], left_b[...], TN, precision=HI, preferred_element_type=jnp.float32)
    start = pl.multiple_of(lax.rem(place_ref[0], 128 // width) * width, width)
    out_ref[...] = scratch[pl.ds(start, width), :]


def gram_slab(place, width, left_a, left_b):
    rows, rank = left_a.shape
    part = pl.BlockSpec((rows, 128), lambda i, p: (0, p[0] // (128 // width)))
    whole = pl.BlockSpec((rows, rank), lambda i, p: (0, 0))
    return call(
        slab_kernel,
        jax.ShapeDtypeStruct((width, rank), jnp.float32),
        (1,),
        [part, part, whole, whole],
        pl.BlockSpec((width, rank), lambda i, p: (0, 0)),
        [pltpu.VMEM((128, rank), jnp.float32)],
        flops=24 * rows * 128 * rank,
        moved=10 * rows * rank,
    )(place.reshape(1), left_a, left_b, left_a, left_b)


def last_kernel(factor, orth_ref, blended_ref, right_ref, colsq_ref, momentum_ref, next_ref, update_ref):
    @pl.when(pl.program_id(0) == 0)
    def _():
        scale = 1.0 / jnp.sqrt(colsq_ref[...] + 1e-06)
        next_ref[...] = (right_ref[...].astype(jnp.float32) * scale).astype(jnp.bfloat16)

    correction = lax.dot_general(orth_ref[...], right_ref[...], NT, preferred_element_type=jnp.float32)
    momentum_ref[...] = (blended_ref[...].astype(jnp.float32) - 0.1 * correction).astype(jnp.bfloat16)
    product = lax.dot_general(orth_ref[...], next_ref[...], NT, preferred_element_type=jnp.float32)
    update_ref[...] = (factor * product).astype(jnp.bfloat16)


def last_products(factor, left_orth, blended, right_bf, colsq):
    rows, cols = blended.shape
    rank = left_orth.shape[1]
    tile = 256
    block = pl.BlockSpec((tile, cols), lambda i: (i, 0))
    whole = pl.BlockSpec((cols, rank), lambda i: (0, 0))
    big = jax.ShapeDtypeStruct((rows, cols), jnp.bfloat16)
    return call(
        lambda *refs: last_kernel(factor, *refs),
        (big, jax.ShapeDtypeStruct((cols, rank), jnp.bfloat16), big),
        (rows // tile,),
        [pl.BlockSpec((tile, rank), lambda i: (i, 0)), block, whole, pl.BlockSpec((1, rank), lambda i: (0, 0))],
        [block, whole, block],
        flops=4 * rows * cols * rank,
        moved=6 * rows * cols + 4 * cols * rank + 2 * rows * rank,
        scalars=0,
        vmem=60 * 1024 * 1024,
    )(left_orth, blended, right_bf, colsq)


def three_terms(value):
    high = lax.reduce_precision(value, 8, 7)
    rest = value - high
    mid = lax.reduce_precision(rest, 8, 7)
    return [t.astype(jnp.bfloat16) for t in (high, mid, rest - mid)]


def swap_cores(value):
    return lax.ppermute(value, "c", [(0, 1), (1, 0)])


def spread_over(value, axes, parts):
    many = jnp.broadcast_to(value[None], (parts,) + value.shape)
    return lax.all_to_all(many, axes, 0, 0, tiled=True)


def gather_over_chips(value, chips):
    return spread_over(value, CHIPS, chips).reshape(chips * value.shape[0], value.shape[1])


def per_device(gradient, momentum, right_factor):
    rows_dev, cols_dev = gradient.shape
    rank = right_factor.shape[1]
    chips = lax.axis_size("x") * lax.axis_size("y")
    depth = lax.axis_size("z")
    core = lax.axis_index("c")
    place = (core * lax.axis_size("x") + lax.axis_index("x")) * lax.axis_size("y") + lax.axis_index("y")
    blended = (momentum.astype(jnp.float32) + gradient.astype(jnp.float32)).astype(jnp.bfloat16)
    half = rows_dev // 2
    part_b, part_a = (
        jnp.dot(
            lax.dynamic_slice_in_dim(blended, h * half, half),
            right_factor,
            preferred_element_type=jnp.float32,
        )
        for h in (1 - core, core)
    )
    part_a = lax.optimization_barrier(part_a)
    pair = (part_a + swap_cores(part_b)).reshape(chips, rows_dev // (2 * chips), rank)
    shard = jnp.sum(lax.all_to_all(pair, CHIPS, 0, 0, tiled=True), axis=0)
    left_a = gather_over_chips(shard, chips)
    left_b = swap_cores(left_a)
    left = lax.dynamic_update_slice(jnp.zeros((rows_dev, rank), jnp.float32), left_a, (core * half, 0))
    left = lax.dynamic_update_slice(left, left_b, ((1 - core) * half, 0))
    wide = sum(
        lax.dot_general(blended, t, TN, preferred_element_type=jnp.float32) for t in three_terms(left)
    )
    wide = lax.psum_scatter(wide, "z", scatter_dimension=0, tiled=True)
    slab = gram_slab(place, rank // (2 * chips), left_a, left_b)
    slab = jnp.sum(spread_over(slab, "z", depth), axis=0)
    mine = gather_over_chips(slab, chips)
    other = swap_cores(mine)
    gram = jnp.concatenate([jnp.where(core == 0, mine, other), jnp.where(core == 0, other, mine)])
    inverse = chol_inverse(gram)
    right = lax.dot_general(wide, inverse, NT, precision=HI, preferred_element_type=jnp.float32)
    colsq = jnp.sum(right * right, axis=0)
    right_bf = lax.all_gather(right.astype(jnp.bfloat16), "z", axis=0, tiled=True)
    left_orth = lax.dot_general(left, inverse, NT, precision=HI, preferred_element_type=jnp.float32).astype(jnp.bfloat16)
    colsq = colsq.reshape(rank // 128, 128)
    colsq = jnp.sum(spread_over(colsq, ("x", "y", "c"), 2 * chips), axis=0)
    colsq = jnp.sum(spread_over(colsq, "z", depth), axis=0).reshape(1, rank)
    factor = (rows_dev * depth * cols_dev * 2 * chips / rank) ** 0.5
    return last_products(factor, left_orth, blended, right_bf, colsq)


def solution(mesh):
    fine = Mesh(mesh.devices.reshape(8, 4, 4, 2), ("z", "x", "y", "c"))
    col = ("x", "y", "c")
    return jax.shard_map(
        per_device,
        mesh=fine,
        in_specs=(P("z", col), P("z", col), P(col, None)),
        out_specs=(P("z", col), P(col, None), P("z", col)),
        check_vma=False,
    )
```

```python
import jax
import jax.numpy as jnp
from jax import lax
from jax.experimental import pallas as pl
from jax.experimental.pallas import tpu as pltpu
from jax.sharding import Mesh, PartitionSpec as P

HI = lax.Precision.HIGHEST
TILE = 8


def diag_inverse(block):
    n = block.shape[0]
    tiles = n // TILE
    shape = (TILE, n)
    row = lax.broadcasted_iota(jnp.int32, shape, 0)
    lane = lax.broadcasted_iota(jnp.int32, shape, 1)
    s = [block[t * TILE:(t + 1) * TILE, :] for t in range(tiles)]
    x = [jnp.where(lane == row + t * TILE, 1.0, 0.0) for t in range(tiles)]
    spread = lambda v, i: jnp.broadcast_to(v[i:i + 1, :], shape)
    for p in range(tiles):
        rest = range(p + 1, tiles)
        col = [
            {t: jnp.broadcast_to(s[t][:, p * TILE + b:p * TILE + b + 1], shape) for t in range(p, tiles)}
            for b in range(TILE)
        ]
        for j in range(TILE):
            inv = lax.rsqrt(spread(col[j][p], j))
            low = {t: col[j][t] * inv for t in range(p, tiles)}
            mult = jnp.where(row > j, low[p], 0.0)
            keep = jnp.where(row == j, inv, 1.0)
            for b in range(j + 1, TILE):
                u = spread(low[p], b)
                for t in range(p, tiles):
                    col[b][t] = col[b][t] - low[t] * u
            srow = spread(s[p], j) * inv
            xrow = spread(x[p], j) * inv
            s[p] = s[p] * keep - mult * srow
            x[p] = x[p] * keep - mult * xrow
            for t in rest:
                s[t] = s[t] - low[t] * srow
                x[t] = x[t] - low[t] * xrow
    return jnp.concatenate(x, axis=0)


def chol_kernel(gram_ref, inv_ref, work):
    n = gram_ref.shape[0]
    nb = 128
    work[...] = gram_ref[...]
    inv_ref[...] = jnp.zeros((n, n), jnp.float32)
    dot = lambda a, b: jnp.dot(a, b, precision=HI, preferred_element_type=jnp.float32)

    def finish(o, d):
        after = o + nb
        here = slice(o, after)
        inv_ref[here, here] = d
        if o:
            inv_ref[here, :o] = dot(d, inv_ref[here, :o])
        if after < n:
            u = dot(d, work[here, after:])
            ut = u.T
            work[after:, after:] = work[after:, after:] - dot(ut, u)
            inv_ref[after:, :after] = inv_ref[after:, :after] - dot(ut, inv_ref[here, :after])

    def step(k, carry):
        o = pl.multiple_of(k * nb, nb)
        d = diag_inverse(work[pl.ds(o, nb), pl.ds(o, nb)])
        for which in range(n // nb):
            pl.when(k == which)(lambda: finish(which * nb, d))
        return carry

    lax.fori_loop(0, n // nb, step, 0)

def chol_inverse(gram):
    n = gram.shape[0]
    return pl.pallas_call(
        chol_kernel,
        out_shape=jax.ShapeDtypeStruct((n, n), jnp.float32),
        in_specs=[pl.BlockSpec(memory_space=pltpu.VMEM)],
        out_specs=pl.BlockSpec(memory_space=pltpu.VMEM),
        scratch_shapes=[pltpu.VMEM((n, n), jnp.float32)],
        compiler_params=pltpu.CompilerParams(vmem_limit_bytes=16 * 1024 * 1024),
        cost_estimate=pl.CostEstimate(flops=20 * 10**9, bytes_accessed=8 * n * n, transcendentals=0),
    )(gram)


CHIPS = ("x", "y")
VMEM = 16 * 1024 * 1024
TN = (((0,), (0,)), ((), ()))
NT = (((1,), (1,)), ((), ()))


def call(kernel, out_shape, grid, in_specs, out_specs, scratch=(), flops=0, moved=0, scalars=1, vmem=VMEM):
    return pl.pallas_call(
        kernel,
        out_shape=out_shape,
        grid_spec=pltpu.PrefetchScalarGridSpec(
            num_scalar_prefetch=scalars, grid=grid, in_specs=in_specs, out_specs=out_specs, scratch_shapes=list(scratch)
        ),
        compiler_params=pltpu.CompilerParams(vmem_limit_bytes=vmem),
        cost_estimate=pl.CostEstimate(flops=flops, bytes_accessed=moved, transcendentals=0),
    )


def slab_kernel(place_ref, part_a, part_b, left_a, left_b, out_ref, scratch):
    width = out_ref.shape[0]
    scratch[...] = lax.dot_general(
        part_a[...], left_a[...], TN, precision=HI, preferred_element_type=jnp.float32
    ) + lax.dot_general(part_b[...], left_b[...], TN, precision=HI, preferred_element_type=jnp.float32)
    start = pl.multiple_of(lax.rem(place_ref[0], 128 // width) * width, width)
    out_ref[...] = scratch[pl.ds(start, width), :]


def gram_slab(place, width, left_a, left_b):
    rows, rank = left_a.shape
    part = pl.BlockSpec((rows, 128), lambda i, p: (0, p[0] // (128 // width)))
    whole = pl.BlockSpec((rows, rank), lambda i, p: (0, 0))
    return call(
        slab_kernel,
        jax.ShapeDtypeStruct((width, rank), jnp.float32),
        (1,),
        [part, part, whole, whole],
        pl.BlockSpec((width, rank), lambda i, p: (0, 0)),
        [pltpu.VMEM((128, rank), jnp.float32)],
        flops=24 * rows * 128 * rank,
        moved=10 * rows * rank,
    )(place.reshape(1), left_a, left_b, left_a, left_b)


def last_kernel(factor, orth_ref, blended_ref, right_ref, colsq_ref, momentum_ref, next_ref, update_ref, scaled):
    step = pl.program_id(0)

    @pl.when(step == 0)
    def _():
        scale = 1.0 / jnp.sqrt(colsq_ref[...] + 1e-06)
        scaled[...] = (right_ref[...].astype(jnp.float32) * scale).astype(jnp.bfloat16)

    piece = next_ref.shape[0]
    next_ref[...] = scaled[pl.ds(pl.multiple_of(step * piece, piece), piece), :]

    correction = lax.dot_general(orth_ref[...], right_ref[...], NT, preferred_element_type=jnp.float32)
    momentum_ref[...] = (blended_ref[...].astype(jnp.float32) - 0.1 * correction).astype(jnp.bfloat16)
    product = lax.dot_general(orth_ref[...], scaled[...], NT, preferred_element_type=jnp.float32)
    update_ref[...] = (factor * product).astype(jnp.bfloat16)


def last_products(factor, left_orth, blended, right_bf, colsq):
    rows, cols = blended.shape
    rank = left_orth.shape[1]
    tile = 256
    block = pl.BlockSpec((tile, cols), lambda i: (i, 0))
    whole = pl.BlockSpec((cols, rank), lambda i: (0, 0))
    big = jax.ShapeDtypeStruct((rows, cols), jnp.bfloat16)
    return call(
        lambda *refs: last_kernel(factor, *refs),
        (big, jax.ShapeDtypeStruct((cols, rank), jnp.bfloat16), big),
        (rows // tile,),
        [pl.BlockSpec((tile, rank), lambda i: (i, 0)), block, whole, pl.BlockSpec((1, rank), lambda i: (0, 0))],
        [block, pl.BlockSpec((cols * tile // rows, rank), lambda i: (i, 0)), block],
        [pltpu.VMEM((cols, rank), jnp.bfloat16)],
        flops=4 * rows * cols * rank,
        moved=6 * rows * cols + 4 * cols * rank + 2 * rows * rank,
        scalars=0,
        vmem=60 * 1024 * 1024,
    )(left_orth, blended, right_bf, colsq)


def three_terms(value):
    high = lax.reduce_precision(value, 8, 7)
    rest = value - high
    mid = lax.reduce_precision(rest, 8, 7)
    return [t.astype(jnp.bfloat16) for t in (high, mid, rest - mid)]


def swap_cores(value):
    return lax.ppermute(value, "c", [(0, 1), (1, 0)])


def spread_over(value, axes, parts):
    many = jnp.broadcast_to(value[None], (parts,) + value.shape)
    return lax.all_to_all(many, axes, 0, 0, tiled=True)


def gather_over_chips(value, chips):
    return spread_over(value, CHIPS, chips).reshape(chips * value.shape[0], value.shape[1])


def per_device(gradient, momentum, right_factor):
    rows_dev, cols_dev = gradient.shape
    rank = right_factor.shape[1]
    chips = lax.axis_size("x") * lax.axis_size("y")
    depth = lax.axis_size("z")
    core = lax.axis_index("c")
    place = (core * lax.axis_size("x") + lax.axis_index("x")) * lax.axis_size("y") + lax.axis_index("y")
    blended = (momentum.astype(jnp.float32) + gradient.astype(jnp.float32)).astype(jnp.bfloat16)
    half = rows_dev // 2
    part_b, part_a = (
        jnp.dot(
            lax.dynamic_slice_in_dim(blended, h * half, half),
            right_factor,
            preferred_element_type=jnp.float32,
        )
        for h in (1 - core, core)
    )
    part_a = lax.optimization_barrier(part_a)
    pair = (part_a + swap_cores(part_b)).reshape(chips, rows_dev // (2 * chips), rank)
    shard = jnp.sum(lax.all_to_all(pair, CHIPS, 0, 0, tiled=True), axis=0)
    left_a = gather_over_chips(shard, chips)
    left_b = swap_cores(left_a)
    left = lax.dynamic_update_slice(jnp.zeros((rows_dev, rank), jnp.float32), left_a, (core * half, 0))
    left = lax.dynamic_update_slice(left, left_b, ((1 - core) * half, 0))
    slab = gram_slab(place, rank // (2 * chips), left_a, left_b)
    wide = sum(
        lax.dot_general(blended, t, TN, preferred_element_type=jnp.float32) for t in three_terms(left)
    )
    slab, wide = lax.optimization_barrier((slab, wide))
    wide = lax.psum_scatter(wide, "z", scatter_dimension=0, tiled=True)
    slab = jnp.sum(spread_over(slab, "z", depth), axis=0)
    mine = gather_over_chips(slab, chips)
    other = swap_cores(mine)
    gram = jnp.concatenate([jnp.where(core == 0, mine, other), jnp.where(core == 0, other, mine)])
    inverse = chol_inverse(gram)
    right = lax.dot_general(wide, inverse, NT, precision=HI, preferred_element_type=jnp.float32)
    colsq = jnp.sum(right * right, axis=0)
    right_bf = lax.all_gather(right.astype(jnp.bfloat16), "z", axis=0, tiled=True)
    left_orth = lax.dot_general(left, inverse, NT, precision=HI, preferred_element_type=jnp.float32).astype(jnp.bfloat16)
    colsq = colsq.reshape(rank // 128, 128)
    colsq = jnp.sum(spread_over(colsq, ("x", "y", "c"), 2 * chips), axis=0)
    colsq = jnp.sum(spread_over(colsq, "z", depth), axis=0).reshape(1, rank)
    factor = (rows_dev * depth * cols_dev * 2 * chips / rank) ** 0.5
    return last_products(factor, left_orth, blended, right_bf, colsq)


def solution(mesh):
    fine = Mesh(mesh.devices.reshape(8, 4, 4, 2), ("z", "x", "y", "c"))
    col = ("x", "y", "c")
    return jax.shard_map(
        per_device,
        mesh=fine,
        in_specs=(P("z", col), P("z", col), P(col, None)),
        out_specs=(P("z", col), P(col, None), P("z", col)),
        check_vma=False,
    )
```

```python
import jax
import jax.numpy as jnp
from jax import lax
from jax.experimental import pallas as pl
from jax.experimental.pallas import tpu as pltpu
from jax.sharding import Mesh, PartitionSpec as P

HI = lax.Precision.HIGHEST
TILE = 8


def diag_inverse(block):
    n = block.shape[0]
    tiles = n // TILE
    shape = (TILE, n)
    row = lax.broadcasted_iota(jnp.int32, shape, 0)
    lane = lax.broadcasted_iota(jnp.int32, shape, 1)
    s = [block[t * TILE:(t + 1) * TILE, :] for t in range(tiles)]
    x = [jnp.where(lane == row + t * TILE, 1.0, 0.0) for t in range(tiles)]
    spread = lambda v, i: jnp.broadcast_to(v[i:i + 1, :], shape)
    for p in range(tiles):
        rest = range(p + 1, tiles)
        col = [
            {t: jnp.broadcast_to(s[t][:, p * TILE + b:p * TILE + b + 1], shape) for t in range(p, tiles)}
            for b in range(TILE)
        ]
        for j in range(TILE):
            inv = lax.rsqrt(spread(col[j][p], j))
            low = {t: col[j][t] * inv for t in range(p, tiles)}
            mult = jnp.where(row > j, low[p], 0.0)
            keep = jnp.where(row == j, inv, 1.0)
            for b in range(j + 1, TILE):
                u = spread(low[p], b)
                for t in range(p, tiles):
                    col[b][t] = col[b][t] - low[t] * u
            srow = spread(s[p], j) * inv
            xrow = spread(x[p], j) * inv
            s[p] = s[p] * keep - mult * srow
            x[p] = x[p] * keep - mult * xrow
            for t in rest:
                s[t] = s[t] - low[t] * srow
                x[t] = x[t] - low[t] * xrow
    return jnp.concatenate(x, axis=0)


def chol_kernel(gram_ref, inv_ref, work):
    n = gram_ref.shape[0]
    nb = 128
    for r in range(0, n, nb):
        work[r:r + nb, r:] = gram_ref[r:r + nb, r:]
    inv_ref[...] = jnp.zeros((n, n), jnp.float32)
    dot = lambda a, b: jnp.dot(a, b, precision=HI, preferred_element_type=jnp.float32)

    def finish(o, d):
        after = o + nb
        here = slice(o, after)
        inv_ref[here, here] = d
        if o:
            inv_ref[here, :o] = dot(d, inv_ref[here, :o])
        if after < n:
            u = dot(d, work[here, after:])
            ut = u.T
            for r in range(after, n, nb):
                below = slice(r, r + nb)
                work[below, r:] = work[below, r:] - dot(ut[r - after:r - after + nb, :], u[:, r - after:])
            inv_ref[after:, :after] = inv_ref[after:, :after] - dot(ut, inv_ref[here, :after])

    def step(k, carry):
        o = pl.multiple_of(k * nb, nb)
        d = diag_inverse(work[pl.ds(o, nb), pl.ds(o, nb)])
        for which in range(n // nb):
            pl.when(k == which)(lambda: finish(which * nb, d))
        return carry

    lax.fori_loop(0, n // nb, step, 0)

def chol_inverse(gram):
    n = gram.shape[0]
    return pl.pallas_call(
        chol_kernel,
        out_shape=jax.ShapeDtypeStruct((n, n), jnp.float32),
        in_specs=[pl.BlockSpec(memory_space=pltpu.VMEM)],
        out_specs=pl.BlockSpec(memory_space=pltpu.VMEM),
        scratch_shapes=[pltpu.VMEM((n, n), jnp.float32)],
        compiler_params=pltpu.CompilerParams(vmem_limit_bytes=16 * 1024 * 1024),
        cost_estimate=pl.CostEstimate(flops=20 * 10**9, bytes_accessed=8 * n * n, transcendentals=0),
    )(gram)


CHIPS = ("x", "y")
VMEM = 16 * 1024 * 1024
TN = (((0,), (0,)), ((), ()))
NT = (((1,), (1,)), ((), ()))


def call(kernel, out_shape, grid, in_specs, out_specs, scratch=(), flops=0, moved=0, scalars=1, vmem=VMEM):
    return pl.pallas_call(
        kernel,
        out_shape=out_shape,
        grid_spec=pltpu.PrefetchScalarGridSpec(
            num_scalar_prefetch=scalars, grid=grid, in_specs=in_specs, out_specs=out_specs, scratch_shapes=list(scratch)
        ),
        compiler_params=pltpu.CompilerParams(vmem_limit_bytes=vmem),
        cost_estimate=pl.CostEstimate(flops=flops, bytes_accessed=moved, transcendentals=0),
    )


def slab_kernel(place_ref, part_a, part_b, left_a, left_b, out_ref, scratch):
    width = out_ref.shape[0]
    scratch[...] = lax.dot_general(
        part_a[...], left_a[...], TN, precision=HI, preferred_element_type=jnp.float32
    ) + lax.dot_general(part_b[...], left_b[...], TN, precision=HI, preferred_element_type=jnp.float32)
    start = pl.multiple_of(lax.rem(place_ref[0], 128 // width) * width, width)
    out_ref[...] = scratch[pl.ds(start, width), :]


def gram_slab(place, width, left_a, left_b):
    rows, rank = left_a.shape
    part = pl.BlockSpec((rows, 128), lambda i, p: (0, p[0] // (128 // width)))
    whole = pl.BlockSpec((rows, rank), lambda i, p: (0, 0))
    return call(
        slab_kernel,
        jax.ShapeDtypeStruct((width, rank), jnp.float32),
        (1,),
        [part, part, whole, whole],
        pl.BlockSpec((width, rank), lambda i, p: (0, 0)),
        [pltpu.VMEM((128, rank), jnp.float32)],
        flops=24 * rows * 128 * rank,
        moved=10 * rows * rank,
    )(place.reshape(1), left_a, left_b, left_a, left_b)


def last_kernel(factor, orth_ref, blended_ref, right_ref, colsq_ref, momentum_ref, next_ref, update_ref, scaled):
    step = pl.program_id(0)

    @pl.when(step == 0)
    def _():
        scale = 1.0 / jnp.sqrt(colsq_ref[...] + 1e-06)
        scaled[...] = (right_ref[...].astype(jnp.float32) * scale).astype(jnp.bfloat16)

    piece = next_ref.shape[0]
    next_ref[...] = scaled[pl.ds(pl.multiple_of(step * piece, piece), piece), :]

    correction = lax.dot_general(orth_ref[...], right_ref[...], NT, preferred_element_type=jnp.float32)
    momentum_ref[...] = (blended_ref[...].astype(jnp.float32) - 0.1 * correction).astype(jnp.bfloat16)
    product = lax.dot_general(orth_ref[...], scaled[...], NT, preferred_element_type=jnp.float32)
    update_ref[...] = (factor * product).astype(jnp.bfloat16)


def last_products(factor, left_orth, blended, right_bf, colsq):
    rows, cols = blended.shape
    rank = left_orth.shape[1]
    tile = 256
    block = pl.BlockSpec((tile, cols), lambda i: (i, 0))
    whole = pl.BlockSpec((cols, rank), lambda i: (0, 0))
    big = jax.ShapeDtypeStruct((rows, cols), jnp.bfloat16)
    return call(
        lambda *refs: last_kernel(factor, *refs),
        (big, jax.ShapeDtypeStruct((cols, rank), jnp.bfloat16), big),
        (rows // tile,),
        [pl.BlockSpec((tile, rank), lambda i: (i, 0)), block, whole, pl.BlockSpec((1, rank), lambda i: (0, 0))],
        [block, pl.BlockSpec((cols * tile // rows, rank), lambda i: (i, 0)), block],
        [pltpu.VMEM((cols, rank), jnp.bfloat16)],
        flops=4 * rows * cols * rank,
        moved=6 * rows * cols + 4 * cols * rank + 2 * rows * rank,
        scalars=0,
        vmem=60 * 1024 * 1024,
    )(left_orth, blended, right_bf, colsq)


def three_terms(value):
    high = lax.reduce_precision(value, 8, 7)
    rest = value - high
    mid = lax.reduce_precision(rest, 8, 7)
    return [t.astype(jnp.bfloat16) for t in (high, mid, rest - mid)]


def swap_cores(value):
    return lax.ppermute(value, "c", [(0, 1), (1, 0)])


def spread_over(value, axes, parts):
    many = jnp.broadcast_to(value[None], (parts,) + value.shape)
    return lax.all_to_all(many, axes, 0, 0, tiled=True)


def gather_over_chips(value, chips):
    return spread_over(value, CHIPS, chips).reshape(chips * value.shape[0], value.shape[1])


def per_device(gradient, momentum, right_factor):
    rows_dev, cols_dev = gradient.shape
    rank = right_factor.shape[1]
    chips = lax.axis_size("x") * lax.axis_size("y")
    depth = lax.axis_size("z")
    core = lax.axis_index("c")
    place = (core * lax.axis_size("x") + lax.axis_index("x")) * lax.axis_size("y") + lax.axis_index("y")
    blended = (momentum.astype(jnp.float32) + gradient.astype(jnp.float32)).astype(jnp.bfloat16)
    half = rows_dev // 2
    part_b, part_a = (
        jnp.dot(
            lax.dynamic_slice_in_dim(blended, h * half, half),
            right_factor,
            preferred_element_type=jnp.float32,
        )
        for h in (1 - core, core)
    )
    part_a = lax.optimization_barrier(part_a)
    pair = (part_a + swap_cores(part_b)).reshape(chips, rows_dev // (2 * chips), rank)
    shard = jnp.sum(lax.all_to_all(pair, CHIPS, 0, 0, tiled=True), axis=0)
    left_a = gather_over_chips(shard, chips)
    left_b = swap_cores(left_a)
    left = lax.dynamic_update_slice(jnp.zeros((rows_dev, rank), jnp.float32), left_a, (core * half, 0))
    left = lax.dynamic_update_slice(left, left_b, ((1 - core) * half, 0))
    slab = gram_slab(place, rank // (2 * chips), left_a, left_b)
    wide = sum(
        lax.dot_general(blended, t, TN, preferred_element_type=jnp.float32) for t in three_terms(left)
    )
    slab, wide = lax.optimization_barrier((slab, wide))
    wide = lax.psum_scatter(wide, "z", scatter_dimension=0, tiled=True)
    slab = jnp.sum(spread_over(slab, "z", depth), axis=0)
    mine = gather_over_chips(slab, chips)
    other = swap_cores(mine)
    gram = jnp.concatenate([jnp.where(core == 0, mine, other), jnp.where(core == 0, other, mine)])
    inverse = chol_inverse(gram)
    right = lax.dot_general(wide, inverse, NT, precision=HI, preferred_element_type=jnp.float32)
    colsq = jnp.sum(right * right, axis=0)
    right_bf = lax.all_gather(right.astype(jnp.bfloat16), "z", axis=0, tiled=True)
    left_orth = lax.dot_general(left, inverse, NT, precision=HI, preferred_element_type=jnp.float32).astype(jnp.bfloat16)
    colsq = colsq.reshape(rank // 128, 128)
    colsq = jnp.sum(spread_over(colsq, ("x", "y", "c"), 2 * chips), axis=0)
    colsq = jnp.sum(spread_over(colsq, "z", depth), axis=0).reshape(1, rank)
    factor = (rows_dev * depth * cols_dev * 2 * chips / rank) ** 0.5
    return last_products(factor, left_orth, blended, right_bf, colsq)


def solution(mesh):
    fine = Mesh(mesh.devices.reshape(8, 4, 4, 2), ("z", "x", "y", "c"))
    col = ("x", "y", "c")
    return jax.shard_map(
        per_device,
        mesh=fine,
        in_specs=(P("z", col), P("z", col), P(col, None)),
        out_specs=(P("z", col), P(col, None), P("z", col)),
        check_vma=False,
    )
```
